512 devices in a mesh: row: 16 (over z_lo, core), col: 16 (over y, x), layer: 2 (over z_hi).
Axes of the slice: x: 4, y: 4, z: 16 (z_hi: 2, z_lo: 8; z = z_hi * 8 + z_lo), core: 2. Of those that a mesh axis runs over, the one named last changes fastest.
Arguments:
- basis: float32 [4096, 4096], P('row', 'col'), may hold values from -1 to 1, as said below
- basis_grad: float32 [4096, 4096], P('row', 'col'), may hold values from -768 to 768
- value_grad: float32 [4096], replicated, may hold values from -384 to 384
- ranks: int32 [4096], replicated, may hold values from 0 to 4095, each once
- offsets: int32 [4096], replicated, may hold values from 0 to 3
Outputs:
- grad_matrix: float32 [4096, 4096], P(('row', 'layer'), 'col')
The draws below stay inside these ranges and needn't reach their ends.
Inputs may be any that keep to these rules, and one draw needn't show every extreme that they name: The columns of basis are orthonormal. ranks holds every number of 0 to 4095 once, so eigenvalues of different indices differ by 1 or more.
All inputs are finite; a program needn't handle non-finite values.
Results may differ from the reference program's by a relative error of at most 0.000098.
Values sent between devices are 32-bit elements; how exact they have to be, the bound alone decides.
No kernel may reach another device: no remote copies, remote signals or barrier semaphores. Data moves between devices by JAX's collectives and lax.ppermute only.
A program may use at most 64 MiB of HBM per device.

```python
import jax
import jax.numpy as jnp
from jax import lax

N = 4096


def draw_basis(key, part):
    source = jax.random.normal(key, (N, N), jnp.float32)
    factor, upper = jnp.linalg.qr(source)
    signs = jnp.where(jnp.diagonal(upper) < 0, -1.0, 1.0)
    return (factor * signs[None, :]).astype(jnp.float32)


def with_ends(values, key, low, largest):
    longest = values.shape.index(max(values.shape))
    spots = []
    for shift in (0, 1):
        where = [jax.random.randint(jax.random.fold_in(key, axis), (), 0, length) for axis, length in enumerate(values.shape)]
        where[longest] = (where[longest] + shift) % values.shape[longest]
        spots.append(tuple(where))
    return values.at[spots[0]].set(low).at[spots[1]].set(largest)


def level_of(key, shape, shards, smallest, high):
    gain = 1.0
    for axis_at, blocks in shards:
        draws = jax.random.uniform(jax.random.fold_in(jax.random.fold_in(key, 6), axis_at), (blocks,), jnp.float32, smallest / len(shards), high / len(shards))
        gain = gain * jnp.repeat(jnp.exp(draws), shape[axis_at] // blocks).reshape((-1,) + (1,) * (len(shape) - 1 - axis_at))
    return gain


def noise(key, extent, width, most, shards=(), kind=jnp.bfloat16):
    drawn = jax.random.normal(key, extent, jnp.float32) * width
    if len(shards) > 0:
        drawn = level_of(key, extent, shards, -0.22, 0.18) * drawn
    return jnp.clip(drawn, min=-most, max=most).astype(kind)


def setup_inputs(seed: int = 0) -> dict:
    key_of = jax.random.split(jax.random.key(seed), 6)
    basis = draw_basis(jax.random.fold_in(key_of[5], 71), 0)
    basis_grad = noise(key_of[1], (N, N), (2 * N ** 0.5), 768.0, ((0, 16), (1, 16)), jnp.float32)
    value_grad = noise(key_of[2], (N,), (N ** 0.5), 384.0, (), jnp.float32)
    ranks = jax.random.permutation(key_of[3], N).astype(jnp.int32)
    offsets = with_ends(jax.random.randint(key_of[4], (N,), 0, 4), jax.random.fold_in(key_of[4], 1), 0, 3).astype(jnp.int32)
    return dict(basis=basis, basis_grad=basis_grad, value_grad=value_grad, ranks=ranks, offsets=offsets)


def reference(basis, basis_grad, value_grad, ranks, offsets):
    highest = lax.Precision.HIGHEST
    eigen = 4.0 * ranks.astype(jnp.float32) + offsets.astype(jnp.float32)
    inner = jnp.dot(basis.T.astype(jnp.float32), basis_grad.astype(jnp.float32), precision=highest, preferred_element_type=jnp.float32)
    index = jnp.arange(N, dtype=jnp.int32)
    on_diagonal = index[:, None] == index[None, :]
    spacing = eigen[None, :] - eigen[:, None]
    scaled = jnp.where(on_diagonal, value_grad[None, :], inner / jnp.where(on_diagonal, jnp.float32(1.0), spacing))
    left_prod = jnp.dot(basis.astype(jnp.float32), scaled.astype(jnp.float32), precision=highest, preferred_element_type=jnp.float32)
    return jnp.dot(left_prod.astype(jnp.float32), basis.T.astype(jnp.float32), precision=highest, preferred_element_type=jnp.float32)
```

```python
import jax
import jax.numpy as jnp
from jax import lax
from jax.sharding import Mesh
from jax.sharding import PartitionSpec as P

AXES = ("zl", "co", "y", "x", "zh")
SIZES = (8, 2, 4, 4, 2)
SHIFT = 3
PREC = lax.Precision.HIGH


def place(z, co, y, x):
    return (((z % 8 * 2 + co) * 4 + y) * 4 + x) * 2 + z // 8


def moved(v, target):
    pairs = [
        (place(z, co, y, x), place(*target(z, co, y, x)))
        for z in range(16)
        for co in range(2)
        for y in range(4)
        for x in range(4)
    ]
    return lax.ppermute(v, AXES, pairs)


def other_core(z, co, y, x):
    return z, 1 - co, y, x


def other_layer(z, co, y, x):
    return (z + 8) % 16, co, y, x


def along(distance):
    def target(z, co, y, x):
        at = (z - SHIFT * co) % 16
        return ((at ^ distance) + SHIFT * co) % 16, co, y, x

    return target


def sent_to_all(v, axis):
    peers = lax.axis_size(axis)
    return lax.all_to_all(jnp.broadcast_to(v[None], (peers, *v.shape)), axis, 0, 0, tiled=True)


def dot(a, b, contract):
    return lax.dot_general(
        a, b, (contract, ((), ())), precision=PREC, preferred_element_type=jnp.float32
    )


def part(v, which, length, dim=0):
    return lax.dynamic_slice_in_dim(v, which * length, length, dim)


def joined(own, other, bit, dim=0):
    return jnp.where(
        bit == 1,
        jnp.concatenate([other, own], dim),
        jnp.concatenate([own, other], dim),
    )


def on_device(basis, basis_grad, value_grad, ranks, offsets):
    n = basis.shape[0]
    quarter = n // 4
    zl, co, y, x, zh = (lax.axis_index(a) for a in AXES)
    z = zh * 8 + zl
    at = (z - SHIFT * co) % 16
    spot = at % 8
    group = at // 8
    group_other = ((z - SHIFT * (1 - co)) % 16) // 8
    bits = [spot % 2, spot // 2 % 2, spot // 4]
    mine = 2 * co + group
    theirs = 2 * (1 - co) + group_other

    turned = jnp.stack([basis_grad.T, basis.T])
    own = part(turned, mine, quarter, 1)
    other = moved(part(turned, theirs, quarter, 1), other_core)
    both = joined(own[:, None], other[:, None], co, 1)

    wide = sent_to_all(basis, "x")
    grads = sent_to_all(both[0], "y")
    wide_other = moved(wide, other_core)

    far = both[1][None]
    for distance, bit in ((4, bits[2]), (2, bits[1]), (1, bits[0])):
        far_got = moved(far, along(distance))
        far = joined(far[:, None], far_got[:, None], bit, 1).reshape(-1, *far.shape[1:])
    far = jnp.where(co == 1, jnp.roll(far, SHIFT, 0), far)
    far = lax.all_to_all(far.reshape(4, 4, quarter, n), "y", 0, 0, tiled=True)
    far = far.swapaxes(0, 1).reshape(4, 4 * quarter, n)

    def grads_of(core):
        return lax.dynamic_index_in_dim(grads, core, 1, False).reshape(4 * quarter, n)

    def flat(w):
        return w.swapaxes(0, 1).reshape(n, 4 * n)

    wide_own = flat(wide)
    wide_oth = flat(wide_other)
    inner = dot(grads_of(co), wide_own, ((1,), (0,))) + dot(
        grads_of(1 - co), wide_oth, ((1,), (0,))
    )
    rows = 4 * quarter
    for distance, bit in ((1, bits[0]), (2, bits[1]), (4, bits[2])):
        rows //= 2
        got = moved(part(inner, 1 - bit, rows), along(distance))
        inner = part(inner, bit, rows) + got

    eigen = 4.0 * ranks.astype(jnp.float32) + offsets.astype(jnp.float32)

    def of_columns(v):
        v = part(part(v.reshape(4, 4, 4, quarter), x, 1, 1), mine, 1, 2).reshape(4 * quarter)
        return lax.dynamic_slice_in_dim(
            v, bits[0] * 8 * rows // 2 + bits[1] * 2 * rows + bits[2] * rows, rows, 0
        )

    index = jnp.arange(eigen.shape[0], dtype=jnp.int32)
    col_index = of_columns(index)
    col_eigen = of_columns(eigen)
    col_grad = of_columns(value_grad)
    row_index = part(index, y, 4 * n)
    row_eigen = part(eigen, y, 4 * n)
    on_diagonal = col_index[:, None] == row_index[None, :]
    spacing = col_eigen[:, None] - row_eigen[None, :]
    scaled = jnp.where(
        on_diagonal,
        col_grad[:, None],
        inner / jnp.where(on_diagonal, jnp.float32(1.0), spacing),
    )
    for distance, bit in ((4, bits[2]), (2, bits[1]), (1, bits[0])):
        got = moved(scaled, along(distance))
        scaled = joined(scaled, got, bit)

    left = joined(
        dot(wide_own, scaled, ((1,), (1,))), dot(wide_oth, scaled, ((1,), (1,))), co
    )
    left = lax.all_to_all(left.reshape(4, n // 2, n), "y", 0, 0, tiled=True).sum(0)
    left = sent_to_all(left, "y").reshape(2, n, n)

    def product(core):
        rows_of = lax.dynamic_index_in_dim(left, core, 0, False)
        return jnp.stack([dot(rows_of, far[i], ((1,), (0,))) for i in range(4)])

    theirs_out = moved(product(1 - co), other_core)
    out = product(co) + theirs_out
    out = lax.all_to_all(out, "x", 0, 0, tiled=True).sum(0)
    return part(out, zh, n // 2) + moved(part(out, 1 - zh, n // 2), other_layer)


def solution(mesh):
    torus = Mesh(mesh.devices.reshape(SIZES), AXES)
    return jax.shard_map(
        on_device,
        mesh=torus,
        in_specs=(P(("zl", "co"), ("y", "x")), P(("zl", "co"), ("y", "x")), P(), P(), P()),
        out_specs=P(("zl", "co", "zh"), ("y", "x")),
        check_vma=False,
    )
```

```python
import jax
import jax.numpy as jnp
from jax import lax
from jax.sharding import Mesh
from jax.sharding import PartitionSpec as P

AXES = ("zl", "co", "y", "x", "zh")
SIZES = (8, 2, 4, 4, 2)
SHIFT = 3
PREC = lax.Precision.HIGH


def place(z, co, y, x):
    return (((z % 8 * 2 + co) * 4 + y) * 4 + x) * 2 + z // 8


def moved(v, target):
    pairs = [
        (place(z, co, y, x), place(*target(z, co, y, x)))
        for z in range(16)
        for co in range(2)
        for y in range(4)
        for x in range(4)
    ]
    return lax.ppermute(v, AXES, pairs)


def other_core(z, co, y, x):
    return z, 1 - co, y, x


def around(step):
    def target(z, co, y, x):
        return z, co, y, (x - step) % 4

    return target


def other_layer(z, co, y, x):
    return (z + 8) % 16, co, y, x


def along(distance):
    def target(z, co, y, x):
        at = (z - SHIFT * co) % 16
        return ((at ^ distance) + SHIFT * co) % 16, co, y, x

    return target


def to_all(v, axis):
    return lax.all_to_all(v, axis, 0, 0, tiled=True)


def sent_to_all(v, axis):
    peers = lax.axis_size(axis)
    return to_all(jnp.broadcast_to(v[None], (peers, *v.shape)), axis)


def dot(a, b, contract=((1,), (0,))):
    return lax.dot_general(
        a, b, (contract, ((), ())), precision=PREC, preferred_element_type=jnp.float32
    )


def tied(*values):
    return lax.optimization_barrier(values)


def part(v, which, length, dim=0):
    return lax.dynamic_slice_in_dim(v, which * length, length, dim)


def turned_round(v, first):
    return lax.dynamic_slice_in_dim(jnp.concatenate([v, v]), first, v.shape[0], 0)


def joined(own, other, bit, dim=0):
    return jnp.where(
        bit == 1,
        jnp.concatenate([other, own], dim),
        jnp.concatenate([own, other], dim),
    )


def on_device(basis, basis_grad, value_grad, ranks, offsets):
    n = basis.shape[0]
    quarter = n // 4
    half = n // 2
    zl, co, y, x, zh = (lax.axis_index(a) for a in AXES)
    z = zh * 8 + zl
    at = (z - SHIFT * co) % 16
    group = at // 8
    group_other = ((z - SHIFT * (1 - co)) % 16) // 8
    bits = [at % 2, at // 2 % 2, at // 4 % 2]
    mine = 2 * co + group
    theirs = 2 * (1 - co) + group_other

    turned = jnp.stack([basis_grad.T, basis.T])
    own = part(turned, mine, quarter, 1)
    other = moved(part(turned, theirs, quarter, 1), other_core)

    wide_own = jnp.stack([basis] + [moved(basis, around(r)) for r in (1, 3, 2)])
    wide_oth = moved(wide_own, other_core)
    slots = [0, 1, 3, 2]

    grads = sent_to_all(jnp.stack([own[0], other[0]]), "y")

    far = joined(own[1][None], other[1][None], co)[None]
    for distance, bit in ((4, bits[2]), (2, bits[1])):
        got = moved(far, along(distance))
        far = joined(far[:, None], got[:, None], bit, 1).reshape(-1, *far.shape[1:])
    wide_oth, far = tied(wide_oth, far)
    got = moved(far, along(1))
    far = joined(far[:, None], got[:, None], bits[0], 1).reshape(-1, *far.shape[1:])

    def flat(w):
        return w.swapaxes(0, 1).reshape(n, 4 * n)

    def inner_of(t):
        g = grads[2 * t : 2 * t + 2]
        return dot(g[:, 0].reshape(half, n), flat(wide_own)) + dot(
            g[:, 1].reshape(half, n), flat(wide_oth)
        )

    inner = [inner_of(t) for t in range(2)]
    rows = half
    for distance, bit in ((1, bits[0]), (2, bits[1]), (4, bits[2])):
        rows //= 2
        for t in range(2):
            got = moved(part(inner[t], 1 - bit, rows), along(distance))
            inner[t] = part(inner[t], bit, rows) + got
        if distance == 1:
            inner[0], far = tied(inner[0], far)
            far = jnp.where(co == 1, jnp.roll(far, SHIFT, 0), far)
            far = to_all(far.reshape(4, 4, quarter, n), "y")
            far = far.swapaxes(1, 2).reshape(4 * quarter, 4 * n)
            w = jnp.concatenate([wide_own, wide_oth], 1).reshape(4, 2, 2, half, n)
            w = jnp.where(zh == 0, w[:, :, ::-1], w)
            upright = w.reshape(4, 2 * n, n).swapaxes(1, 2).reshape(4 * n, 2 * n)

    eigen = 4.0 * ranks.astype(jnp.float32) + offsets.astype(jnp.float32)
    index = jnp.arange(eigen.shape[0], dtype=jnp.int32)

    def of_columns(v):
        return part(part(v.reshape(4, 4, 4, quarter), x, 1, 1), mine, 1, 2).reshape(4 * quarter)

    def of_rows(v):
        v = turned_round(part(v.reshape(4, 4, n), y, 1)[0], x)
        return jnp.stack([v[r] for r in slots]).reshape(4 * n)

    row_index, row_eigen = of_rows(index), of_rows(eigen)
    columns = [of_columns(v) for v in (index, eigen, value_grad)]
    scaled = []
    for t in range(2):
        begin = t * half + (bits[0] * 4 + bits[1] * 2 + bits[2]) * rows
        col_index, col_eigen, col_grad = (
            lax.dynamic_slice_in_dim(v, begin, rows, 0)[:, None] for v in columns
        )
        on_diagonal = col_index == row_index[None, :]
        spacing = jnp.where(on_diagonal, jnp.float32(1.0), col_eigen - row_eigen[None, :])
        scaled.append(jnp.where(on_diagonal, col_grad, inner[t] / spacing))
    scaled[0], far, upright = tied(scaled[0], far, upright)
    for distance, bit in ((4, bits[2]), (2, bits[1]), (1, bits[0])):
        for t in range(2):
            got = moved(scaled[t], along(distance))
            scaled[t] = joined(scaled[t], got, bit)

    left = []
    for t in range(2):
        term = dot(scaled[t], upright)
        term = to_all(term.reshape(4, half // 4, 2 * n), "y").sum(0)
        left.append(sent_to_all(term, "y").reshape(half, 2 * n))

    def product(block):
        at_block = slice(block * half, (block + 1) * half)
        out = sum(
            dot(left[t][:, at_block], far[t * half : (t + 1) * half], ((0,), (0,)))
            for t in range(2)
        )
        return out.reshape(half, 4, n).swapaxes(0, 1)

    def summed(v):
        return to_all(v, "x").sum(0)

    leaving = moved(product(2), other_core)
    staying = moved(product(3), other_core)
    leaving = moved(summed(product(0) + leaving), other_layer)
    return summed(product(1) + staying) + leaving


def solution(mesh):
    torus = Mesh(mesh.devices.reshape(SIZES), AXES)
    return jax.shard_map(
        on_device,
        mesh=torus,
        in_specs=(P(("zl", "co"), ("y", "x")), P(("zl", "co"), ("y", "x")), P(), P(), P()),
        out_specs=P(("zl", "co", "zh"), ("y", "x")),
        check_vma=False,
    )
```

```python
import jax
import jax.numpy as jnp
from jax import lax
from jax.sharding import Mesh
from jax.sharding import PartitionSpec as P

AXES = ("zl", "co", "y", "x", "zh")
SIZES = (8, 2, 4, 4, 2)
SHIFT = 3
PREC = lax.Precision.HIGH


def place(z, co, y, x):
    return (((z % 8 * 2 + co) * 4 + y) * 4 + x) * 2 + z // 8


def moved(v, target):
    pairs = [
        (place(z, co, y, x), place(*target(z, co, y, x)))
        for z in range(16)
        for co in range(2)
        for y in range(4)
        for x in range(4)
    ]
    return lax.ppermute(v, AXES, pairs)


def other_core(z, co, y, x):
    return z, 1 - co, y, x


def other_layer(z, co, y, x):
    return (z + 8) % 16, co, y, x


def along(distance):
    def target(z, co, y, x):
        at = (z - SHIFT * co) % 16
        return ((at ^ distance) + SHIFT * co) % 16, co, y, x

    return target


def to_all(v, axis):
    return lax.all_to_all(v, axis, 0, 0, tiled=True)


def sent_to_all(v, axis):
    peers = lax.axis_size(axis)
    return to_all(jnp.broadcast_to(v[None], (peers, *v.shape)), axis)


def turned_round(v, first):
    return lax.dynamic_slice_in_dim(jnp.concatenate([v, v]), first, v.shape[0], 0)


def dot(a, b, contract=((1,), (0,))):
    return lax.dot_general(
        a, b, (contract, ((), ())), precision=PREC, preferred_element_type=jnp.float32
    )


def tied(*values):
    return lax.optimization_barrier(values)


def part(v, which, length, dim=0):
    return lax.dynamic_slice_in_dim(v, which * length, length, dim)


def joined(own, other, bit, dim=0):
    return jnp.where(
        bit == 1,
        jnp.concatenate([other, own], dim),
        jnp.concatenate([own, other], dim),
    )


def on_device(basis, basis_grad, value_grad, ranks, offsets):
    n = basis.shape[0]
    quarter = n // 4
    half = n // 2
    zl, co, y, x, zh = (lax.axis_index(a) for a in AXES)
    z = zh * 8 + zl
    at = (z - SHIFT * co) % 16
    group = at // 8
    group_other = ((z - SHIFT * (1 - co)) % 16) // 8
    bits = [at % 2, at // 2 % 2, at // 4 % 2]
    mine = 2 * co + group
    theirs = 2 * (1 - co) + group_other

    turned = jnp.stack([basis_grad.T, basis.T])
    own = part(turned, mine, quarter, 1)
    other = moved(part(turned, theirs, quarter, 1), other_core)

    wide = sent_to_all(basis, "x")
    grads = jnp.broadcast_to(jnp.stack([own[0], other[0]])[None], (4, 2, quarter, n))
    far = joined(own[1][None], other[1][None], co)
    far = joined(far[None], moved(far, along(4))[None], bits[2])
    wide, grads, far = tied(wide, grads, far)
    (wide,) = tied(wide.swapaxes(0, 1).reshape(n, 4 * n))
    wide_oth = moved(wide, other_core)
    grads = to_all(grads, "y")

    far = joined(far[:, None], moved(far, along(2))[:, None], bits[1], 1)
    grads, far = tied(grads, far.reshape(4, 2, quarter, n))
    far = turned_round(far, (4 - co * ((SHIFT + bits[0]) // 2)) % 4)

    def inner_of(which):
        g = part(grads, which, 2)
        return dot(g[:, 0].reshape(half, n), wide) + dot(g[:, 1].reshape(half, n), wide_oth)

    got = moved(inner_of(1 - bits[0]), along(1))
    kept = inner_of(bits[0])
    rows = half
    for distance, bit in ((2, bits[1]), (4, bits[2])):
        rows //= 2
        leaving = part(kept, 1 - bit, rows) + part(got, 1 - bit, rows)
        kept = part(kept, bit, rows) + part(got, bit, rows)
        got = moved(leaving, along(distance))
    inner = kept + got

    eigen = 4.0 * ranks.astype(jnp.float32) + offsets.astype(jnp.float32)
    index = jnp.arange(eigen.shape[0], dtype=jnp.int32)

    def of_columns(v):
        v = part(part(v.reshape(4, 4, 4, quarter), x, 1, 1), mine, 1, 2).reshape(4 * quarter)
        return part(v, bits[0] * 4 + bits[1] * 2 + bits[2], rows)[:, None]

    row_index, row_eigen = (part(v, y, 4 * n)[None, :] for v in (index, eigen))
    on_diagonal = of_columns(index) == row_index
    spacing = jnp.where(on_diagonal, jnp.float32(1.0), of_columns(eigen) - row_eigen)
    scaled = jnp.where(on_diagonal, of_columns(value_grad), inner / spacing)

    scaled, far = tied(scaled, far)
    far = to_all(far, "y")
    for distance, bit in ((4, bits[2]), (2, bits[1])):
        scaled = joined(scaled, moved(scaled, along(distance)), bit)
    scaled_oth = moved(scaled, along(1))

    def left_of(s):
        return jnp.concatenate([dot(w, s, ((1,), (1,))) for w in (wide, wide_oth)])

    left = jnp.concatenate([left_of(scaled), left_of(scaled_oth)], 1)
    left, far = tied(left, far)
    far_oth = moved(far, along(1))
    left = to_all(left.reshape(4, half, n), "y").sum(0)
    left = sent_to_all(left, "y").reshape(2 * n, n)

    far = joined(far[None], far_oth[None], z % 2)
    far = far.transpose(1, 3, 0, 2, 4).reshape(2, half, 4 * n)
    (far,) = tied(jnp.where(bits[0] == 1, jnp.stack([far[1], far[0]]), far).reshape(n, 4 * n))

    def product(rows_of):
        return dot(rows_of, far).reshape(n, 4, n).swapaxes(0, 1)

    theirs_out = moved(product(left[n:]), other_core)
    out = to_all(product(left[:n]) + theirs_out, "x").sum(0)
    return part(out, zh, half) + moved(part(out, 1 - zh, half), other_layer)


def solution(mesh):
    torus = Mesh(mesh.devices.reshape(SIZES), AXES)
    return jax.shard_map(
        on_device,
        mesh=torus,
        in_specs=(P(("zl", "co"), ("y", "x")), P(("zl", "co"), ("y", "x")), P(), P(), P()),
        out_specs=P(("zl", "co", "zh"), ("y", "x")),
        check_vma=False,
    )
```

```python
import jax
import jax.numpy as jnp
from jax import lax
from jax.sharding import Mesh
from jax.sharding import PartitionSpec as P

AXES = ("zq", "zp", "co", "y", "x", "zh")
SIZES = (4, 2, 2, 4, 4, 2)
SHIFT = 3
PREC = lax.Precision.HIGH


def place(z, co, y, x):
    return (((z % 8 * 2 + co) * 4 + y) * 4 + x) * 2 + z // 8


def moved(v, target):
    pairs = [
        (place(z, co, y, x), place(*target(z, co, y, x)))
        for z in range(16)
        for co in range(2)
        for y in range(4)
        for x in range(4)
    ]
    return lax.ppermute(v, AXES, pairs)


def other_core(z, co, y, x):
    return z, 1 - co, y, x


def other_layer(z, co, y, x):
    return (z + 8) % 16, co, y, x


def along(distance):
    def target(z, co, y, x):
        at = (z - SHIFT * co) % 16
        return ((at ^ distance) + SHIFT * co) % 16, co, y, x

    return target


def to_all(v, axis):
    return lax.all_to_all(v, axis, 0, 0, tiled=True)


def sent_to_all(v, axis):
    peers = lax.axis_size(axis)
    return to_all(jnp.broadcast_to(v[None], (peers, *v.shape)), axis)


def dot(a, b, contract=((1,), (0,))):
    return lax.dot_general(
        a, b, (contract, ((), ())), precision=PREC, preferred_element_type=jnp.float32
    )


def tied(*values):
    return lax.optimization_barrier(values)


def part(v, which, length, dim=0):
    return lax.dynamic_slice_in_dim(v, which * length, length, dim)


def joined(own, other, bit, dim=0):
    return jnp.where(
        bit == 1,
        jnp.concatenate([other, own], dim),
        jnp.concatenate([own, other], dim),
    )


def on_device(basis, basis_grad, value_grad, ranks, offsets):
    n = basis.shape[0]
    quarter = n // 4
    half = n // 2
    zq, zp, co, y, x, zh = (lax.axis_index(a) for a in AXES)
    z = zh * 8 + zq * 2 + zp
    at = (z - SHIFT * co) % 16
    group = at // 8
    group_other = ((z - SHIFT * (1 - co)) % 16) // 8
    bits = [at % 2, at // 2 % 2, at // 4 % 2]
    mine = 2 * co + group
    theirs = 2 * (1 - co) + group_other

    def shares(of_grads, core):
        return jnp.concatenate(
            [part(basis_grad.T, of_grads, quarter), part(basis.T, core, half)]
        )

    own = shares(mine, co)
    other = moved(shares(theirs, 1 - co), other_core)

    wide = sent_to_all(basis, "x")
    grads = jnp.broadcast_to(
        jnp.stack([own[:quarter], other[:quarter]])[None], (4, 2, quarter, n)
    )
    far = joined(own[None, quarter:], other[None, quarter:], co).reshape(2, 2, quarter, n)
    grads, far = tied(grads, far)
    far = lax.all_gather(far, "zq")
    wide, grads = tied(wide, grads)
    (wide,) = tied(wide.swapaxes(0, 1).reshape(n, 4 * n))
    wide_oth = moved(wide, other_core)
    grads = to_all(grads, "y")

    def inner_of(which):
        g = part(grads, which, 2)
        return dot(g[:, 0].reshape(half, n), wide) + dot(g[:, 1].reshape(half, n), wide_oth)

    got = moved(inner_of(1 - bits[0]), along(1))
    kept = inner_of(bits[0])
    rows = half
    for distance, bit in ((2, bits[1]), (4, bits[2])):
        rows //= 2
        leaving = part(kept, 1 - bit, rows) + part(got, 1 - bit, rows)
        kept = part(kept, bit, rows) + part(got, bit, rows)
        got = moved(leaving, along(distance))
    inner = kept + got

    eigen = 4.0 * ranks.astype(jnp.float32) + offsets.astype(jnp.float32)
    index = jnp.arange(eigen.shape[0], dtype=jnp.int32)

    def of_columns(v):
        v = part(part(v.reshape(4, 4, 4, quarter), x, 1, 1), mine, 1, 2).reshape(4 * quarter)
        return part(v, bits[0] * 4 + bits[1] * 2 + bits[2], rows)[:, None]

    row_index, row_eigen = (part(v, y, 4 * n)[None, :] for v in (index, eigen))
    on_diagonal = of_columns(index) == row_index
    spacing = jnp.where(on_diagonal, jnp.float32(1.0), of_columns(eigen) - row_eigen)
    scaled = jnp.where(on_diagonal, of_columns(value_grad), inner / spacing)

    scaled = joined(scaled, moved(scaled, along(4)), bits[2])
    scaled = joined(scaled, moved(scaled, along(2)), bits[1])
    scaled, far = tied(scaled, far)
    far = to_all(lax.dynamic_index_in_dim(far, group, 2, False), "y")
    scaled_oth = moved(scaled, along(1))

    def left_of(s):
        return jnp.concatenate([dot(w, s, ((1,), (1,))) for w in (wide, wide_oth)])

    left = jnp.concatenate([left_of(scaled), left_of(scaled_oth)], 1)
    left, far = tied(left, far)
    far_oth = moved(far, along(1))
    left = to_all(left.reshape(4, half, n), "y").sum(0)
    left = sent_to_all(left, "y").reshape(2 * n, n)

    far = joined(far[None], far_oth[None], z % 2)
    far = far.transpose(1, 3, 0, 2, 4).reshape(2, half, 4 * n)
    (far,) = tied(jnp.where(bits[0] == 1, jnp.stack([far[1], far[0]]), far).reshape(n, 4 * n))

    def product(rows_of):
        return dot(rows_of, far).reshape(n, 4, n).swapaxes(0, 1)

    theirs_out = moved(product(left[n:]), other_core)
    out = product(left[:n]) + theirs_out
    leaving = to_all(part(out, 1 - zh, half, 1), "x").sum(0)
    staying, leaving = tied(part(out, zh, half, 1), leaving)
    staying = to_all(staying, "x")
    return staying.sum(0) + moved(leaving, other_layer)


def solution(mesh):
    torus = Mesh(mesh.devices.reshape(SIZES), AXES)
    return jax.shard_map(
        on_device,
        mesh=torus,
        in_specs=(P(("zq", "zp", "co"), ("y", "x")), P(("zq", "zp", "co"), ("y", "x")), P(), P(), P()),
        out_specs=P(("zq", "zp", "co", "zh"), ("y", "x")),
        check_vma=False,
    )
```

```python
import jax
import jax.numpy as jnp
from jax import lax
from jax.sharding import Mesh
from jax.sharding import PartitionSpec as P

AXES = ("zl", "co", "y", "x", "zh")
SIZES = (8, 2, 4, 4, 2)
SHIFT = 3
PREC = lax.Precision.HIGH


def place(z, co, y, x):
    return (((z % 8 * 2 + co) * 4 + y) * 4 + x) * 2 + z // 8


def moved(v, target):
    pairs = [
        (place(z, co, y, x), place(*target(z, co, y, x)))
        for z in range(16)
        for co in range(2)
        for y in range(4)
        for x in range(4)
    ]
    return lax.ppermute(v, AXES, pairs)


def other_core(z, co, y, x):
    return z, 1 - co, y, x


def other_layer(z, co, y, x):
    return (z + 8) % 16, co, y, x


def along(distance):
    def target(z, co, y, x):
        at = (z - SHIFT * co) % 16
        return ((at ^ distance) + SHIFT * co) % 16, co, y, x

    return target


def to_all(v, axis):
    return lax.all_to_all(v, axis, 0, 0, tiled=True)


def sent_to_all(v, axis):
    peers = lax.axis_size(axis)
    return to_all(jnp.broadcast_to(v[None], (peers, *v.shape)), axis)


def turned_round(v, first):
    return lax.dynamic_slice_in_dim(jnp.concatenate([v, v]), first, v.shape[0], 0)


def dot(a, b, contract=((1,), (0,))):
    return lax.dot_general(
        a, b, (contract, ((), ())), precision=PREC, preferred_element_type=jnp.float32
    )


def tied(*values):
    return lax.optimization_barrier(values)


def part(v, which, length, dim=0):
    return lax.dynamic_slice_in_dim(v, which * length, length, dim)


def joined(own, other, bit, dim=0):
    return jnp.where(
        bit == 1,
        jnp.concatenate([other, own], dim),
        jnp.concatenate([own, other], dim),
    )


def on_device(basis, basis_grad, value_grad, ranks, offsets):
    n = basis.shape[0]
    quarter = n // 4
    half = n // 2
    zl, co, y, x, zh = (lax.axis_index(a) for a in AXES)
    z = zh * 8 + zl
    at = (z - SHIFT * co) % 16
    group = at // 8
    group_other = ((z - SHIFT * (1 - co)) % 16) // 8
    bits = [at % 2, at // 2 % 2, at // 4 % 2]
    mine = 2 * co + group
    theirs = 2 * (1 - co) + group_other

    turned = jnp.stack([basis_grad.T, basis.T])
    own = part(turned, mine, quarter, 1)
    other = moved(part(turned, theirs, quarter, 1), other_core)

    wide = sent_to_all(basis, "x")
    grads = jnp.broadcast_to(jnp.stack([own[0], other[0]])[None], (4, 2, quarter, n))

    far = joined(own[1][None], other[1][None], co)
    far = joined(far[None], moved(far, along(4))[None], bits[2])
    wide, grads, far = tied(wide, grads, far)
    (wide,) = tied(wide.swapaxes(0, 1).reshape(n, 4 * n))
    wide_oth = moved(wide, other_core)
    grads = to_all(grads, "y")
    far = joined(far[:, None], moved(far, along(2))[:, None], bits[1], 1)
    grads, far = tied(grads, far.reshape(4, 2, quarter, n))

    def inner_of(which):
        g = part(grads, which, 2)
        return dot(g[:, 0].reshape(half, n), wide) + dot(g[:, 1].reshape(half, n), wide_oth)

    got = moved(inner_of(1 - bits[0]), along(1))
    kept = inner_of(bits[0])
    far = turned_round(far, (4 - co * ((SHIFT + bits[0]) // 2)) % 4)
    rows = half
    for distance, bit in ((2, bits[1]), (4, bits[2])):
        rows //= 2
        leaving = part(kept, 1 - bit, rows) + part(got, 1 - bit, rows)
        kept = part(kept, bit, rows) + part(got, bit, rows)
        got = moved(leaving, along(distance))
    inner = kept + got

    eigen = 4.0 * ranks.astype(jnp.float32) + offsets.astype(jnp.float32)
    index = jnp.arange(eigen.shape[0], dtype=jnp.int32)

    def of_columns(v):
        v = part(part(v.reshape(4, 4, 4, quarter), x, 1, 1), mine, 1, 2).reshape(4 * quarter)
        return part(v, bits[0] * 4 + bits[1] * 2 + bits[2], rows)[:, None]

    row_index, row_eigen = (part(v, y, 4 * n)[None, :] for v in (index, eigen))
    on_diagonal = of_columns(index) == row_index
    spacing = jnp.where(on_diagonal, jnp.float32(1.0), of_columns(eigen) - row_eigen)
    scaled = jnp.where(on_diagonal, of_columns(value_grad), inner / spacing)

    scaled, far = tied(scaled, far)
    far = to_all(far, "y")
    for distance, bit in ((4, bits[2]), (2, bits[1])):
        scaled = joined(scaled, moved(scaled, along(distance)), bit)
    scaled_oth = moved(scaled, along(1))

    def left_of(s):
        terms = [dot(w, s, ((1,), (1,))).reshape(2, half, half) for w in (wide, wide_oth)]
        return to_all(jnp.concatenate(terms), "y")

    left = left_of(scaled)
    scaled_oth, left, far = tied(scaled_oth, left, far)
    far_oth = moved(far, along(1))
    left = jnp.concatenate([left.sum(0), left_of(scaled_oth).sum(0)], 1)
    left = sent_to_all(left, "y")

    far = joined(far[None], far_oth[None], z % 2)
    far = far.transpose(1, 3, 0, 2, 4).reshape(2, half, 4 * n)
    (far,) = tied(jnp.where(bits[0] == 1, jnp.stack([far[1], far[0]]), far).reshape(n, 4 * n))

    def product(core, which):
        rows_of = lax.dynamic_index_in_dim(left, 2 * core + which, 0, False)
        return dot(rows_of, far).reshape(half, 4, n).swapaxes(0, 1)

    leaving = product(0, 1 - zh) + moved(product(1, 1 - zh), other_core)
    leaving = to_all(leaving, "x").sum(0)
    staying, leaving = tied(moved(product(1, zh), other_core), leaving)
    return to_all(product(0, zh) + staying, "x").sum(0) + moved(leaving, other_layer)


def solution(mesh):
    torus = Mesh(mesh.devices.reshape(SIZES), AXES)
    return jax.shard_map(
        on_device,
        mesh=torus,
        in_specs=(P(("zl", "co"), ("y", "x")), P(("zl", "co"), ("y", "x")), P(), P(), P()),
        out_specs=P(("zl", "co", "zh"), ("y", "x")),
        check_vma=False,
    )
```

```python
import jax
import jax.numpy as jnp
from jax import lax
from jax.sharding import Mesh
from jax.sharding import PartitionSpec as P

AXES = ("zl", "co", "y", "x", "zh")
SIZES = (8, 2, 4, 4, 2)
SHIFT = 3
PREC = lax.Precision.HIGH


def place(z, co, y, x):
    return (((z % 8 * 2 + co) * 4 + y) * 4 + x) * 2 + z // 8


def moved(v, target):
    pairs = [
        (place(z, co, y, x), place(*target(z, co, y, x)))
        for z in range(16)
        for co in range(2)
        for y in range(4)
        for x in range(4)
    ]
    return lax.ppermute(v, AXES, pairs)


def other_core(z, co, y, x):
    return z, 1 - co, y, x


def other_layer(z, co, y, x):
    return (z + 8) % 16, co, y, x


def along(distance):
    def target(z, co, y, x):
        at = (z - SHIFT * co) % 16
        return ((at ^ distance) + SHIFT * co) % 16, co, y, x

    return target


def to_all(v, axis):
    return lax.all_to_all(v, axis, 0, 0, tiled=True)


def sent_to_all(v, axis):
    peers = lax.axis_size(axis)
    return to_all(jnp.broadcast_to(v[None], (peers, *v.shape)), axis)


def turned_round(v, first):
    return lax.dynamic_slice_in_dim(jnp.concatenate([v, v]), first, v.shape[0], 0)


def dot(a, b, contract=((1,), (0,))):
    return lax.dot_general(
        a, b, (contract, ((), ())), precision=PREC, preferred_element_type=jnp.float32
    )


def tied(*values):
    return lax.optimization_barrier(values)


def part(v, which, length, dim=0):
    return lax.dynamic_slice_in_dim(v, which * length, length, dim)


def joined(own, other, bit, dim=0):
    return jnp.where(
        bit == 1,
        jnp.concatenate([other, own], dim),
        jnp.concatenate([own, other], dim),
    )


def on_device(basis, basis_grad, value_grad, ranks, offsets):
    n = basis.shape[0]
    quarter = n // 4
    half = n // 2
    zl, co, y, x, zh = (lax.axis_index(a) for a in AXES)
    z = zh * 8 + zl
    at = (z - SHIFT * co) % 16
    group = at // 8
    group_other = ((z - SHIFT * (1 - co)) % 16) // 8
    bits = [at % 2, at // 2 % 2, at // 4 % 2]
    mine = 2 * co + group
    theirs = 2 * (1 - co) + group_other

    turned = jnp.stack([basis_grad.T, basis.T])
    own = part(turned, mine, quarter, 1)
    other = moved(part(turned, theirs, quarter, 1), other_core)

    wide = sent_to_all(basis, "x")
    grads = jnp.broadcast_to(jnp.stack([own[0], other[0]])[None], (4, 2, quarter, n))
    far = joined(own[1][None], other[1][None], co)
    far = joined(far[None], moved(far, along(4))[None], bits[2])
    wide, grads, far = tied(wide, grads, far)
    (wide,) = tied(wide.swapaxes(0, 1).reshape(n, 4 * n))
    wide_oth = moved(wide, other_core)
    grads = to_all(grads, "y")

    far_got = moved(far, along(2))

    def inner_of(which):
        g = part(grads, which, 2)
        return dot(g[:, 0].reshape(half, n), wide) + dot(g[:, 1].reshape(half, n), wide_oth)

    got = moved(inner_of(1 - bits[0]), along(1))
    kept, far_got = tied(inner_of(bits[0]), far_got)
    rows = half
    for distance, bit in ((2, bits[1]), (4, bits[2])):
        rows //= 2
        leaving = part(kept, 1 - bit, rows) + part(got, 1 - bit, rows)
        kept = part(kept, bit, rows) + part(got, bit, rows)
        got = moved(leaving, along(distance))
    inner = kept + got

    eigen = 4.0 * ranks.astype(jnp.float32) + offsets.astype(jnp.float32)
    index = jnp.arange(eigen.shape[0], dtype=jnp.int32)

    def of_columns(v):
        v = part(part(v.reshape(4, 4, 4, quarter), x, 1, 1), mine, 1, 2).reshape(4 * quarter)
        return part(v, bits[0] * 4 + bits[1] * 2 + bits[2], rows)[:, None]

    row_index, row_eigen = (part(v, y, 4 * n)[None, :] for v in (index, eigen))
    on_diagonal = of_columns(index) == row_index
    spacing = jnp.where(on_diagonal, jnp.float32(1.0), of_columns(eigen) - row_eigen)
    scaled = jnp.where(on_diagonal, of_columns(value_grad), inner / spacing)

    far = joined(far[:, None], far_got[:, None], bits[1], 1).reshape(4, 2, quarter, n)
    far = turned_round(far, (4 - co * ((SHIFT + bits[0]) // 2)) % 4)
    scaled, far = tied(scaled, far)
    far = to_all(far, "y")
    for distance, bit in ((4, bits[2]), (2, bits[1])):
        scaled = joined(scaled, moved(scaled, along(distance)), bit)
    scaled_oth = moved(scaled, along(1))

    def left_of(s):
        return jnp.concatenate([dot(w, s, ((1,), (1,))) for w in (wide, wide_oth)])

    left = jnp.concatenate([left_of(scaled), left_of(scaled_oth)], 1)
    left, far = tied(left, far)
    far_oth = moved(far, along(1))
    left = to_all(left.reshape(4, half, n), "y").sum(0)
    left = sent_to_all(left, "y").reshape(2 * n, n)

    far = joined(far[None], far_oth[None], z % 2)
    far = far.transpose(1, 3, 0, 2, 4).reshape(2, half, 4 * n)
    (far,) = tied(jnp.where(bits[0] == 1, jnp.stack([far[1], far[0]]), far).reshape(n, 4 * n))

    def product(rows_of):
        return dot(rows_of, far).reshape(n, 4, n).swapaxes(0, 1)

    theirs_out = moved(product(left[n:]), other_core)
    out = to_all(product(left[:n]) + theirs_out, "x").sum(0)
    return part(out, zh, half) + moved(part(out, 1 - zh, half), other_layer)


def solution(mesh):
    torus = Mesh(mesh.devices.reshape(SIZES), AXES)
    return jax.shard_map(
        on_device,
        mesh=torus,
        in_specs=(P(("zl", "co"), ("y", "x")), P(("zl", "co"), ("y", "x")), P(), P(), P()),
        out_specs=P(("zl", "co", "zh"), ("y", "x")),
        check_vma=False,
    )
```
